32 devices in a mesh: seq: 2 (over x), mp: 4 (over z), dp: 4 (over y, core).
Axes of the slice: x: 2, y: 2, z: 4, core: 2. Of those that a mesh axis runs over, the one named last changes fastest.
Arguments:
- query: bfloat16 [2048, 4096], P(('dp', 'seq'), 'mp'), parts along dimension 0, may hold values from -6 to 6
- key: bfloat16 [2048, 4096], P(('dp', 'seq'), 'mp'), parts along dimension 0, may hold values from -6 to 6
- value: bfloat16 [2048, 4096], P(('dp', 'seq'), 'mp'), parts along dimension 0, may hold values from -6 to 6
- out_weight: bfloat16 [4096, 6144], P('seq', 'mp'), may hold values from -1.5 to 1.5
- lengths: int32 [48], P('dp'), parts along dimension 0, may hold values from 1 to 384, 512 in all
- grad_out: bfloat16 [2048, 6144], P(('dp', 'seq'), 'mp'), parts along dimension 0, may hold values from -0.29882812 to 0.29882812
Outputs:
- mixed: bfloat16 [2048, 6144], P(('dp', 'seq'), 'mp'), parts along dimension 0
- grad_query: bfloat16 [2048, 4096], P(('dp', 'seq'), 'mp'), parts along dimension 0
- grad_key: bfloat16 [2048, 4096], P(('dp', 'seq'), 'mp'), parts along dimension 0
- grad_value: bfloat16 [2048, 4096], P(('dp', 'seq'), 'mp'), parts along dimension 0
- grad_weight: bfloat16 [16384, 6144], P(('dp', 'seq'), 'mp'), parts along dimension 0
The draws below stay inside these ranges and needn't reach their ends.
There are 4 independent parts, one for each index of `dp`. The reference program is written for one: setup_inputs(seed, part) draws one part's arguments, and reference() takes and returns one part's arrays. A program takes and returns all parts, laid end to end along the dimension named above; an argument that names none is the same for every part. Nothing has to cross between parts.
Inputs may be any that keep to these rules, and one draw needn't show every extreme that they name: The images lie end to end from position 0 and their lengths sum to 512.
All inputs are finite; a program needn't handle non-finite values.
Results may differ from the reference program's by a relative error of at most 0.025.
Values may be sent and summed in bfloat16 or wider, within the bound.
A program may use at most 128 MiB of HBM per device.

```python
import math
import jax
import jax.numpy as jnp
import numpy as np
from jax import lax

D = 6144
HEAD_DIM = 128
IMAGES = 12
SEQ_LEN = 512
MAXLEN = 384
HQ = 4096


def draw_query(key, part):
    key = jax.random.fold_in(key, 11)
    result = jax.random.truncated_normal(key, -6.0, 6.0, (SEQ_LEN, HQ), jnp.float32)
    return result.astype(jnp.bfloat16)


def draw_key(key, part):
    key = jax.random.fold_in(key, 23)
    result = jax.random.truncated_normal(key, -6.0, 6.0, (SEQ_LEN, HQ), jnp.float32)
    return result.astype(jnp.bfloat16)


def block_scale(key, dims, cuts, smallest, largest):
    factor_of = 1.0
    for axis_at, shards_of in cuts:
        draws = jax.random.uniform(jax.random.fold_in(jax.random.fold_in(key, 6), axis_at), (shards_of,), jnp.float32, smallest / len(cuts), largest / len(cuts))
        factor_of = factor_of * jnp.repeat(jnp.exp(draws), dims[axis_at] // shards_of).reshape((-1,) + (1,) * (len(dims) - 1 - axis_at))
    return factor_of


def length_profile(count, total, most, lean):
    weights = [(1 << 20) // math.isqrt(rank ** lean) + 1 for rank in range(2, count + 1)]
    spare, given = total - most - (count - 1), [1] * (count - 1)
    while spare > 0:
        free = [i for i in range(count - 1) if given[i] < most]
        mass, left = sum([weights[i] for i in free]), spare
        for i in free:
            more = min(most - given[i], max(1, left * weights[i] // mass), spare)
            given[i] = given[i] + more
            spare = spare - more
    return np.array([most] + given)


def ragged_sizes(own_key, number_of, total, most, slope):
    if number_of == 2:
        one = jax.random.randint(own_key, (), max(1, total - most), min(most, total - 1) + 1)
        return jnp.stack([one, total - one])
    sizes = jnp.asarray(length_profile(number_of, total, most, slope), jnp.int32)
    twos = (number_of - 1) // 2
    source_of, receiver = sizes[1:1 + 2 * twos:2], sizes[2:2 + 2 * twos:2]
    room = jnp.minimum(source_of - 1, most - receiver)
    moved = jax.random.randint(jax.random.fold_in(own_key, 1), (twos,), 0, 1 << 20) % (room + 1)
    sizes = sizes.at[1:1 + 2 * twos:2].set(source_of - moved).at[2:2 + 2 * twos:2].set(receiver + moved)
    return sizes[jax.random.permutation(jax.random.fold_in(own_key, 2), number_of)]


def centred(own_key, extent, width, bound, cuts=(), kind=jnp.bfloat16):
    factor_of = block_scale(own_key, extent, cuts, -0.22, 0.18) if cuts else 1.0
    array = jax.random.normal(own_key, extent, jnp.float32) * width * factor_of
    return jnp.minimum(jnp.maximum(array, -bound), bound).astype(kind)


def setup_inputs(seed: int = 0, part: int = 0) -> dict:
    arg_keys = jax.random.split(jax.random.key(seed), 7)
    part_keys = jax.random.split(jax.random.fold_in(arg_keys[6], part), 7)
    return {
        "query": draw_query(jax.random.fold_in(jax.random.fold_in(arg_keys[6], part), 71), part),
        "key": draw_key(jax.random.fold_in(jax.random.fold_in(arg_keys[6], part), 71), part),
        "value": centred(part_keys[2], (SEQ_LEN, HQ), 1.0, 6.0, ((0, 2), (1, 4))),
        "out_weight": centred(arg_keys[3], (HQ, D), (HQ // 256) ** -0.5, 1.5, ((0, 2), (1, 4))),
        "lengths": ragged_sizes(part_keys[4], IMAGES, SEQ_LEN, MAXLEN, 2).astype(jnp.int32),
        "grad_out": centred(part_keys[5], (SEQ_LEN, D), 0.05, 0.29882812, ((0, 2), (1, 4))),
    }


def image_ids(lengths, count):
    ends = jnp.cumsum(lengths).astype(jnp.int32)
    places = jnp.arange(count, dtype=jnp.int32)
    return jnp.sum((places[:, None] >= ends[None, :]).astype(jnp.int32), axis=1)


def reference(query, key, value, out_weight, lengths, grad_out):
    seq_total = query.shape[0]
    width_all = query.shape[1]
    heads = width_all // HEAD_DIM
    scale = HEAD_DIM ** -0.5
    ids = image_ids(lengths, seq_total)
    same = ids[:, None] == ids[None, :]

    def split(arr):
        return arr.reshape(seq_total, heads, HEAD_DIM).transpose(1, 0, 2)

    def join(arr):
        return arr.transpose(1, 0, 2).reshape(seq_total, width_all)

    q_heads, k_heads, v_heads = split(query), split(key), split(value)

    def forward_head(items):
        q_one, k_one, v_one = items
        score = jnp.dot(q_one, k_one.T, preferred_element_type=jnp.float32) * scale
        score = jnp.where(same, score, -1e30)
        top = jnp.max(score, axis=1)
        weights = jnp.where(same, jnp.exp(score - top[:, None]), 0.0)
        total = jnp.sum(weights, axis=1)
        summed = jnp.dot(weights.astype(jnp.bfloat16), v_one, preferred_element_type=jnp.float32)
        return (summed / total[:, None]).astype(jnp.bfloat16), top + jnp.log(total)

    attn_heads, stats = lax.map(forward_head, (q_heads, k_heads, v_heads))
    attention = join(attn_heads)
    mixed = jnp.dot(attention, out_weight, preferred_element_type=jnp.float32).astype(jnp.bfloat16)
    d_attention = jnp.dot(grad_out, out_weight.T, preferred_element_type=jnp.float32).astype(jnp.bfloat16)
    grad_weight = jnp.dot(attention.T, grad_out, preferred_element_type=jnp.float32).astype(jnp.bfloat16)
    d_heads = split(d_attention)
    deltas = jnp.sum(d_heads.astype(jnp.float32) * attn_heads.astype(jnp.float32), axis=2)

    def backward_head(items):
        q_one, k_one, v_one, d_one, stat, delta = items
        score = jnp.dot(q_one, k_one.T, preferred_element_type=jnp.float32) * scale
        score = jnp.where(same, score, -1e30)
        prob = jnp.exp(score - stat[:, None])
        d_v = jnp.dot(prob.astype(jnp.bfloat16).T, d_one, preferred_element_type=jnp.float32)
        d_p = jnp.dot(d_one, v_one.T, preferred_element_type=jnp.float32)
        d_score = (prob * (d_p - delta[:, None])).astype(jnp.bfloat16)
        d_q = jnp.dot(d_score, k_one, preferred_element_type=jnp.float32) * scale
        d_k = jnp.dot(d_score.T, q_one, preferred_element_type=jnp.float32) * scale
        return d_q.astype(jnp.bfloat16), d_k.astype(jnp.bfloat16), d_v.astype(jnp.bfloat16)

    g_q, g_k, g_v = lax.map(backward_head, (q_heads, k_heads, v_heads, d_heads, stats, deltas))
    return mixed, join(g_q), join(g_k), join(g_v), grad_weight
```

```python
import math

import jax
import jax.numpy as jnp
from jax import lax
from jax.experimental import pallas as pl
from jax.experimental.pallas import tpu as pltpu
from jax.sharding import PartitionSpec as P

HEAD_DIM = 128


HEADS_IN_ALL = 32
NEG = -1e30


def image_ids(ends, first, count):
    places = first + jnp.arange(count, dtype=jnp.int32)
    return jnp.sum((places[:, None] >= ends[None, :]).astype(jnp.int32), axis=1)


def body(query, key, value, out_weight, lengths, grad_out):
    tok_rows, width = query.shape
    heads = width // HEAD_DIM
    scale = HEAD_DIM ** (-0.5)
    ends = jnp.cumsum(lengths)
    first_row = lax.axis_index("seq") * tok_rows
    query_ids = image_ids(ends, first_row, tok_rows)
    every_q, every_k, every_v = (
        lax.all_gather(query, "seq", axis=0, tiled=True),
        lax.all_gather(key, "seq", axis=0, tiled=True),
        lax.all_gather(value, "seq", axis=0, tiled=True),
    )
    seq_total = every_k.shape[0]
    block = math.gcd(512, seq_total)
    steps_all = jnp.arange(seq_total // block, dtype=jnp.int32)
    local_q = query.reshape(tok_rows, heads, HEAD_DIM)
    local_k = key.reshape(tok_rows, heads, HEAD_DIM)
    local_v = value.reshape(tok_rows, heads, HEAD_DIM)

    def key_block(index):
        begin = index * block
        keys = lax.dynamic_slice_in_dim(every_k, begin, block, 0).reshape(block, heads, HEAD_DIM)
        vals = lax.dynamic_slice_in_dim(every_v, begin, block, 0).reshape(block, heads, HEAD_DIM)
        return (keys, vals, image_ids(ends, begin, block))

    def masked_scores(left, right, left_ids, right_ids):
        same = left_ids[:, None] == right_ids[None, :]
        score = jnp.einsum("qhd,khd->hqk", left, right, preferred_element_type=jnp.float32) * scale
        return (jnp.where(same[None], score, NEG), same)

    def forward_step(carry, index):
        keys, vals, key_ids = key_block(index)
        top, total, acc = carry
        score, same = masked_scores(local_q, keys, query_ids, key_ids)
        new_top = jnp.maximum(top, jnp.max(score, axis=2))
        weights = jnp.where(same[None], jnp.exp(score - new_top[:, :, None]), 0.0)
        fade = jnp.exp(top - new_top)
        total = total * fade + jnp.sum(weights, axis=2)
        acc = acc * fade[:, :, None] + jnp.einsum(
            "hqk,khd->hqd", weights.astype(jnp.bfloat16), vals, preferred_element_type=jnp.float32
        )
        carry = (new_top, total, acc)
        return (carry, None)

    start_state = (
        jnp.full((heads, tok_rows), NEG, jnp.float32),
        jnp.zeros((heads, tok_rows), jnp.float32),
        jnp.zeros((heads, tok_rows, HEAD_DIM), jnp.float32),
    )
    (top, total, acc), unused = lax.scan(forward_step, start_state, steps_all)
    attn_local = (acc / total[:, :, None]).astype(jnp.bfloat16)
    stats = top + jnp.log(total)
    attention = attn_local.transpose(1, 0, 2).reshape(tok_rows, width)
    every_heads = lax.all_gather(attention, "mp", axis=1, tiled=True)
    weight_full = lax.all_gather(out_weight, "seq", axis=0, tiled=True)
    mixed = jnp.dot(every_heads, weight_full, preferred_element_type=jnp.float32).astype(
        jnp.bfloat16
    )
    rows = weight_full
    d_attention = (
        lax.psum_scatter(
            lax.dot_general(
                rows, grad_out, (((1,), (1,)), ((), ())), preferred_element_type=jnp.float32
            ).astype(jnp.bfloat16),
            "mp",
            scatter_dimension=0,
            tiled=True,
        )
        .astype(jnp.float32)
        .T.astype(jnp.bfloat16)
    )
    token_heads = lax.all_to_all(every_heads, "seq", split_axis=1, concat_axis=0, tiled=True)
    rows = token_heads
    grad_weight = lax.dot_general(
        rows,
        lax.all_gather(grad_out, "seq", axis=0, tiled=True),
        (((0,), (0,)), ((), ())),
        preferred_element_type=jnp.float32,
    ).astype(jnp.bfloat16)
    d_local = d_attention.reshape(tok_rows, heads, HEAD_DIM)
    deltas = jnp.sum(
        d_local.astype(jnp.float32)
        * attention.reshape(tok_rows, heads, HEAD_DIM).astype(jnp.float32),
        axis=2,
    ).T

    def query_step(summed, index):
        keys, vals, key_ids = key_block(index)
        score, same = masked_scores(local_q, keys, query_ids, key_ids)
        prob = jnp.exp(score - stats[:, :, None])
        d_p = jnp.einsum("qhd,khd->hqk", d_local, vals, preferred_element_type=jnp.float32)
        d_score = (prob * (d_p - deltas[:, :, None])).astype(jnp.bfloat16)
        summed = summed + jnp.einsum(
            "hqk,khd->qhd", d_score, keys, preferred_element_type=jnp.float32
        )
        return (summed, None)

    dq_sum, unused = lax.scan(
        query_step, jnp.zeros((tok_rows, heads, HEAD_DIM), jnp.float32), steps_all
    )
    grad_query = (dq_sum * scale).reshape(tok_rows, width).astype(jnp.bfloat16)
    d_piece = lax.all_gather(d_attention.astype(jnp.float32), "seq", axis=0, tiled=True)
    stat_piece = lax.all_gather(stats.T, "seq", axis=0, tiled=True)
    delta_piece = lax.all_gather(deltas.T, "seq", axis=0, tiled=True)
    count = d_piece.shape[0]
    far_q = every_q.reshape(count, heads, HEAD_DIM)
    far_ids = image_ids(ends, jnp.int32(0), count)
    d_far = d_piece.astype(jnp.bfloat16).reshape(count, heads, HEAD_DIM)
    score, same = masked_scores(far_q, local_k, far_ids, query_ids)
    prob = jnp.exp(score - stat_piece.T[:, :, None])
    acc_v = jnp.einsum(
        "hqk,qhd->khd", prob.astype(jnp.bfloat16), d_far, preferred_element_type=jnp.float32
    )
    d_p = jnp.einsum("qhd,khd->hqk", d_far, local_v, preferred_element_type=jnp.float32)
    d_score = (prob * (d_p - delta_piece.T[:, :, None])).astype(jnp.bfloat16)
    acc_k = jnp.einsum("hqk,qhd->khd", d_score, far_q, preferred_element_type=jnp.float32)
    grad_key = (acc_k * scale).reshape(tok_rows, width).astype(jnp.bfloat16)
    grad_value = acc_v.reshape(tok_rows, width).astype(jnp.bfloat16)
    return (mixed, grad_query, grad_key, grad_value, grad_weight)


def masked_softmax(q, k, row_ids, col_ids):
    score = lax.dot_general(q, k, (((1,), (1,)), ((), ())), preferred_element_type=jnp.float32)
    score = score * HEAD_DIM ** (-0.5)
    same = row_ids == col_ids
    score = jnp.where(same, score, NEG)
    top = jnp.max(score, axis=1, keepdims=True)
    weights = jnp.where(same, jnp.exp(score - top), 0.0)
    return weights, jnp.sum(weights, axis=1, keepdims=True)


def joined(own, far):
    return jnp.concatenate([own[...], far[...]], axis=0)


def forward_kernel(me, rid, cid, qo, qf, ko, kf, vo, vf, out):
    weights, total = masked_softmax(joined(qo, qf), joined(ko, kf), rid[...], cid[...])
    acc = jnp.dot(weights.astype(jnp.bfloat16), joined(vo, vf), preferred_element_type=jnp.float32)
    out[...] = (acc / total).astype(jnp.bfloat16)


def backward_kernel(me, rid, cid, qo, qf, ko, kf, vo, vf, att, datt, *outs):
    q, k, v = joined(qo, qf), joined(ko, kf), joined(vo, vf)
    d_out = datt[...]
    weights, total = masked_softmax(q, k, rid[...], cid[...])
    prob = weights * (1.0 / total)
    delta = jnp.sum(
        d_out.astype(jnp.float32) * att[...].astype(jnp.float32), axis=1, keepdims=True
    )
    d_v = lax.dot_general(
        prob.astype(jnp.bfloat16), d_out, (((0,), (0,)), ((), ())),
        preferred_element_type=jnp.float32,
    )
    d_p = lax.dot_general(d_out, v, (((1,), (1,)), ((), ())), preferred_element_type=jnp.float32)
    d_score = (prob * (d_p - delta)).astype(jnp.bfloat16)
    scale = HEAD_DIM ** (-0.5)
    d_q = jnp.dot(d_score, k, preferred_element_type=jnp.float32) * scale
    d_k = lax.dot_general(
        d_score, q, (((0,), (0,)), ((), ())), preferred_element_type=jnp.float32
    ) * scale
    rows = qo.shape[0]
    for grad, own, far in ((d_q, 0, 1), (d_k, 2, 3), (d_v, 4, 5)):
        outs[own][...] = grad[:rows].astype(jnp.bfloat16)
        outs[far][...] = grad[rows:].astype(jnp.bfloat16)


def attention_call(kernel, me, ids, pairs, extra, split_out):
    rows = pairs[0][1].shape[0]
    width = pairs[0][1].shape[1]
    heads = width // HEAD_DIM
    own = pl.BlockSpec((rows, HEAD_DIM), lambda h, me: (0, me[0] * heads + h))
    far = pl.BlockSpec((rows, HEAD_DIM), lambda h, me: (0, h))
    both = pl.BlockSpec((2 * rows, HEAD_DIM), lambda h, me: (0, h))
    whole = [
        pl.BlockSpec((2 * rows, 1), lambda h, me: (0, 0)),
        pl.BlockSpec((1, 2 * rows), lambda h, me: (0, 0)),
    ]
    if split_out:
        out_specs = [far] * 6
        out_shape = [jax.ShapeDtypeStruct((rows, width), jnp.bfloat16)] * 6
    else:
        out_specs = both
        out_shape = jax.ShapeDtypeStruct((2 * rows, width), jnp.bfloat16)
    matmuls = 5 if split_out else 2
    cells = 4 * rows * rows * heads
    return pl.pallas_call(
        kernel,
        grid_spec=pltpu.PrefetchScalarGridSpec(
            num_scalar_prefetch=1,
            grid=(heads,),
            in_specs=whole + [own, far] * 3 + [both] * len(extra),
            out_specs=out_specs,
        ),
        out_shape=out_shape,
        cost_estimate=pl.CostEstimate(
            flops=cells * 2 * HEAD_DIM * matmuls * 4,
            bytes_accessed=2 * rows * width * 2 * (4 + len(extra) + (3 if split_out else 0)),
            transcendentals=cells,
        ),
        compiler_params=pltpu.CompilerParams(vmem_limit_bytes=48 << 20),
    )(me, ids[:, None], ids[None, :], *[a for pair in pairs for a in pair], *extra)


def dot_f32(a, b, left, right):
    return lax.dot_general(a, b, (((left,), (right,)), ((), ())), preferred_element_type=jnp.float32)


def paired_body(query, key, value, out_weight, lengths, grad_out):
    rows, width = query.shape
    half = width // 2
    groups = lax.axis_size("mp")
    side = groups // 2
    me = lax.axis_index("seq")
    swap = lambda a: lax.ppermute(a, "seq", [(0, 1), (1, 0)])
    first = me == 0
    ends = jnp.cumsum(lengths)
    ids = jnp.concatenate(
        [image_ids(ends, me * rows, rows), image_ids(ends, (1 - me) * rows, rows)]
    )

    def away(a):
        return lax.dynamic_slice_in_dim(a, (1 - me) * half, half, 1)

    far_q, far_k, far_v = swap(away(query)), swap(away(key)), swap(away(value))
    far_go = swap(grad_out)
    features = out_weight.shape[1]
    weight = out_weight.reshape(side, 2, half, features)
    w_mine = lax.dynamic_index_in_dim(weight, me, 1, keepdims=False).reshape(side * half, features)
    w_away = lax.dynamic_index_in_dim(weight, 1 - me, 1, keepdims=False).reshape(
        side * half, features
    )

    bf = jnp.bfloat16
    cross_own = swap(dot_f32(grad_out, w_away, 1, 1).astype(bf))
    keep_own = dot_f32(grad_out, w_mine, 1, 1).astype(bf)
    cross_far = swap(dot_f32(far_go, w_away, 1, 1).astype(bf))
    keep_far = dot_f32(far_go, w_mine, 1, 1).astype(bf)
    keep = jnp.concatenate([keep_own, keep_far], 0).reshape(2 * rows, side, half)
    got = jnp.concatenate([cross_far, cross_own], 0).reshape(2 * rows, side, half)
    keep, got = keep.transpose(1, 0, 2), got.transpose(1, 0, 2)
    parts = jnp.concatenate([jnp.where(first, keep, got), jnp.where(first, got, keep)], 0)
    d_attention = lax.psum_scatter(
        parts.reshape(groups * 2 * rows, half), "mp", scatter_dimension=0, tiled=True
    )

    pairs = ((query, far_q), (key, far_k), (value, far_v))
    where_me = jnp.reshape(me, (1,)).astype(jnp.int32)
    attention = attention_call(forward_kernel, where_me, ids, pairs, (), False)
    every = lax.all_gather(attention, "mp", axis=0, tiled=False)
    mine = lax.dynamic_slice_in_dim(every, me * side, side, 0)
    theirs = swap(lax.dynamic_slice_in_dim(every, (1 - me) * side, side, 0))

    def beside(a, b):
        return jnp.stack([jnp.where(first, a, b), jnp.where(first, b, a)], 1)

    mine_own, mine_far = mine[:, :rows], mine[:, rows:]
    their_own, their_far = theirs[:, rows:], theirs[:, :rows]
    att_own = beside(mine_own, their_own)
    att_far = beside(mine_far, their_far)

    def project(att):
        return lax.dot_general(
            att, weight, (((0, 1, 3), (0, 1, 2)), ((), ())), preferred_element_type=jnp.float32
        )

    other = swap(project(att_far).astype(bf))
    mixed = (project(att_own) + other.astype(jnp.float32)).astype(bf)
    att_all = jnp.concatenate([att_own, att_far], 2)
    go_all = jnp.concatenate([grad_out, far_go], 0)
    grad_weight = lax.dot_general(
        att_all, go_all, (((2,), (0,)), ((), ())), preferred_element_type=jnp.float32
    ).astype(bf).reshape(out_weight.shape)

    grads = attention_call(
        backward_kernel, where_me, ids, pairs, (attention, d_attention), True
    )

    def home(own, far):
        got = swap(far)
        return jnp.concatenate([jnp.where(first, own, got), jnp.where(first, got, own)], 1)

    grad_query = home(grads[0], grads[1])
    grad_key = home(grads[2], grads[3])
    grad_value = home(grads[4], grads[5])
    return (mixed, grad_query, grad_key, grad_value, grad_weight)


def solution(mesh):
    placed = (
        P(("dp", "seq"), "mp"),
        P(("dp", "seq"), "mp"),
        P(("dp", "seq"), "mp"),
        P("seq", "mp"),
        P("dp"),
        P(("dp", "seq"), "mp"),
    )
    heads_here = HEADS_IN_ALL // mesh.shape["mp"]
    paired = mesh.shape["seq"] == 2 and mesh.shape["mp"] % 2 == 0 and heads_here % 2 == 0
    return jax.shard_map(
        paired_body if paired else body,
        mesh=mesh,
        in_specs=placed,
        out_specs=(
            P(("dp", "seq"), "mp"),
            P(("dp", "seq"), "mp"),
            P(("dp", "seq"), "mp"),
            P(("dp", "seq"), "mp"),
            P(("dp", "seq"), "mp"),
        ),
        check_vma=False,
    )
```

```python
import math

import jax
import jax.numpy as jnp
from jax import lax
from jax.experimental import pallas as pl
from jax.experimental.pallas import tpu as pltpu
from jax.sharding import PartitionSpec as P

HEAD_DIM = 128


HEADS_IN_ALL = 32
NEG = -1e30


def image_ids(ends, first, count):
    places = first + jnp.arange(count, dtype=jnp.int32)
    return jnp.sum((places[:, None] >= ends[None, :]).astype(jnp.int32), axis=1)


def body(query, key, value, out_weight, lengths, grad_out):
    tok_rows, width = query.shape
    heads = width // HEAD_DIM
    scale = HEAD_DIM ** (-0.5)
    ends = jnp.cumsum(lengths)
    first_row = lax.axis_index("seq") * tok_rows
    query_ids = image_ids(ends, first_row, tok_rows)
    every_q, every_k, every_v = (
        lax.all_gather(query, "seq", axis=0, tiled=True),
        lax.all_gather(key, "seq", axis=0, tiled=True),
        lax.all_gather(value, "seq", axis=0, tiled=True),
    )
    seq_total = every_k.shape[0]
    block = math.gcd(512, seq_total)
    steps_all = jnp.arange(seq_total // block, dtype=jnp.int32)
    local_q = query.reshape(tok_rows, heads, HEAD_DIM)
    local_k = key.reshape(tok_rows, heads, HEAD_DIM)
    local_v = value.reshape(tok_rows, heads, HEAD_DIM)

    def key_block(index):
        begin = index * block
        keys = lax.dynamic_slice_in_dim(every_k, begin, block, 0).reshape(block, heads, HEAD_DIM)
        vals = lax.dynamic_slice_in_dim(every_v, begin, block, 0).reshape(block, heads, HEAD_DIM)
        return (keys, vals, image_ids(ends, begin, block))

    def masked_scores(left, right, left_ids, right_ids):
        same = left_ids[:, None] == right_ids[None, :]
        score = jnp.einsum("qhd,khd->hqk", left, right, preferred_element_type=jnp.float32) * scale
        return (jnp.where(same[None], score, NEG), same)

    def forward_step(carry, index):
        keys, vals, key_ids = key_block(index)
        top, total, acc = carry
        score, same = masked_scores(local_q, keys, query_ids, key_ids)
        new_top = jnp.maximum(top, jnp.max(score, axis=2))
        weights = jnp.where(same[None], jnp.exp(score - new_top[:, :, None]), 0.0)
        fade = jnp.exp(top - new_top)
        total = total * fade + jnp.sum(weights, axis=2)
        acc = acc * fade[:, :, None] + jnp.einsum(
            "hqk,khd->hqd", weights.astype(jnp.bfloat16), vals, preferred_element_type=jnp.float32
        )
        carry = (new_top, total, acc)
        return (carry, None)

    start_state = (
        jnp.full((heads, tok_rows), NEG, jnp.float32),
        jnp.zeros((heads, tok_rows), jnp.float32),
        jnp.zeros((heads, tok_rows, HEAD_DIM), jnp.float32),
    )
    (top, total, acc), unused = lax.scan(forward_step, start_state, steps_all)
    attn_local = (acc / total[:, :, None]).astype(jnp.bfloat16)
    stats = top + jnp.log(total)
    attention = attn_local.transpose(1, 0, 2).reshape(tok_rows, width)
    every_heads = lax.all_gather(attention, "mp", axis=1, tiled=True)
    weight_full = lax.all_gather(out_weight, "seq", axis=0, tiled=True)
    mixed = jnp.dot(every_heads, weight_full, preferred_element_type=jnp.float32).astype(
        jnp.bfloat16
    )
    rows = weight_full
    d_attention = (
        lax.psum_scatter(
            lax.dot_general(
                rows, grad_out, (((1,), (1,)), ((), ())), preferred_element_type=jnp.float32
            ).astype(jnp.bfloat16),
            "mp",
            scatter_dimension=0,
            tiled=True,
        )
        .astype(jnp.float32)
        .T.astype(jnp.bfloat16)
    )
    token_heads = lax.all_to_all(every_heads, "seq", split_axis=1, concat_axis=0, tiled=True)
    rows = token_heads
    grad_weight = lax.dot_general(
        rows,
        lax.all_gather(grad_out, "seq", axis=0, tiled=True),
        (((0,), (0,)), ((), ())),
        preferred_element_type=jnp.float32,
    ).astype(jnp.bfloat16)
    d_local = d_attention.reshape(tok_rows, heads, HEAD_DIM)
    deltas = jnp.sum(
        d_local.astype(jnp.float32)
        * attention.reshape(tok_rows, heads, HEAD_DIM).astype(jnp.float32),
        axis=2,
    ).T

    def query_step(summed, index):
        keys, vals, key_ids = key_block(index)
        score, same = masked_scores(local_q, keys, query_ids, key_ids)
        prob = jnp.exp(score - stats[:, :, None])
        d_p = jnp.einsum("qhd,khd->hqk", d_local, vals, preferred_element_type=jnp.float32)
        d_score = (prob * (d_p - deltas[:, :, None])).astype(jnp.bfloat16)
        summed = summed + jnp.einsum(
            "hqk,khd->qhd", d_score, keys, preferred_element_type=jnp.float32
        )
        return (summed, None)

    dq_sum, unused = lax.scan(
        query_step, jnp.zeros((tok_rows, heads, HEAD_DIM), jnp.float32), steps_all
    )
    grad_query = (dq_sum * scale).reshape(tok_rows, width).astype(jnp.bfloat16)
    d_piece = lax.all_gather(d_attention.astype(jnp.float32), "seq", axis=0, tiled=True)
    stat_piece = lax.all_gather(stats.T, "seq", axis=0, tiled=True)
    delta_piece = lax.all_gather(deltas.T, "seq", axis=0, tiled=True)
    count = d_piece.shape[0]
    far_q = every_q.reshape(count, heads, HEAD_DIM)
    far_ids = image_ids(ends, jnp.int32(0), count)
    d_far = d_piece.astype(jnp.bfloat16).reshape(count, heads, HEAD_DIM)
    score, same = masked_scores(far_q, local_k, far_ids, query_ids)
    prob = jnp.exp(score - stat_piece.T[:, :, None])
    acc_v = jnp.einsum(
        "hqk,qhd->khd", prob.astype(jnp.bfloat16), d_far, preferred_element_type=jnp.float32
    )
    d_p = jnp.einsum("qhd,khd->hqk", d_far, local_v, preferred_element_type=jnp.float32)
    d_score = (prob * (d_p - delta_piece.T[:, :, None])).astype(jnp.bfloat16)
    acc_k = jnp.einsum("hqk,qhd->khd", d_score, far_q, preferred_element_type=jnp.float32)
    grad_key = (acc_k * scale).reshape(tok_rows, width).astype(jnp.bfloat16)
    grad_value = acc_v.reshape(tok_rows, width).astype(jnp.bfloat16)
    return (mixed, grad_query, grad_key, grad_value, grad_weight)


def masked_softmax(q, k, row_ids, col_ids):
    score = lax.dot_general(q, k, (((1,), (1,)), ((), ())), preferred_element_type=jnp.float32)
    score = score * HEAD_DIM ** (-0.5)
    same = row_ids == col_ids
    score = jnp.where(same, score, NEG)
    top = jnp.max(score, axis=1, keepdims=True)
    weights = jnp.exp(score - top)
    return weights, jnp.sum(weights, axis=1, keepdims=True)


def joined(own, far):
    return jnp.concatenate([own[...], far], axis=0)


def forward_kernel(me, rid, cid, qo, ko, vo, far, out):
    qf, kf, vf = far[0], far[1], far[2]
    weights, total = masked_softmax(joined(qo, qf), joined(ko, kf), rid[...], cid[...])
    acc = jnp.dot(weights.astype(jnp.bfloat16), joined(vo, vf), preferred_element_type=jnp.float32)
    out[...] = (acc / total).astype(jnp.bfloat16)


def backward_kernel(me, rid, cid, qo, ko, vo, far, att, datt, own_out, far_out):
    qf, kf, vf = far[0], far[1], far[2]
    q, k, v = joined(qo, qf), joined(ko, kf), joined(vo, vf)
    d_out = datt[...]
    weights, total = masked_softmax(q, k, rid[...], cid[...])
    prob = weights * (1.0 / total)
    delta = jnp.sum(
        d_out.astype(jnp.float32) * att[...].astype(jnp.float32), axis=1, keepdims=True
    )
    d_v = lax.dot_general(
        prob.astype(jnp.bfloat16), d_out, (((0,), (0,)), ((), ())),
        preferred_element_type=jnp.float32,
    )
    d_p = lax.dot_general(d_out, v, (((1,), (1,)), ((), ())), preferred_element_type=jnp.float32)
    d_score = (prob * (d_p - delta)).astype(jnp.bfloat16)
    scale = HEAD_DIM ** (-0.5)
    d_q = jnp.dot(d_score, k, preferred_element_type=jnp.float32) * scale
    d_k = lax.dot_general(
        d_score, q, (((0,), (0,)), ((), ())), preferred_element_type=jnp.float32
    ) * scale
    rows = qo.shape[0]
    for i, grad in enumerate((d_q, d_k, d_v)):
        own_out[i] = grad[:rows].astype(jnp.bfloat16)
        far_out[i] = grad[rows:].astype(jnp.bfloat16)


def attention_call(kernel, me, ids, owns, fars, extra, split_out):
    rows, width = fars.shape[1:]
    heads = width // HEAD_DIM
    own = pl.BlockSpec((rows, HEAD_DIM), lambda h, me: (0, me[0] * heads + h))
    far = pl.BlockSpec((3, rows, HEAD_DIM), lambda h, me: (0, 0, h))
    both = pl.BlockSpec((2 * rows, HEAD_DIM), lambda h, me: (0, h))
    whole = [
        pl.BlockSpec((2 * rows, 1), lambda h, me: (0, 0)),
        pl.BlockSpec((1, 2 * rows), lambda h, me: (0, 0)),
    ]
    if split_out:
        out_specs = [far] * 2
        out_shape = [jax.ShapeDtypeStruct((3, rows, width), jnp.bfloat16)] * 2
    else:
        out_specs = both
        out_shape = jax.ShapeDtypeStruct((2 * rows, width), jnp.bfloat16)
    matmuls = 5 if split_out else 2
    cells = 4 * rows * rows * heads
    return pl.pallas_call(
        kernel,
        grid_spec=pltpu.PrefetchScalarGridSpec(
            num_scalar_prefetch=1,
            grid=(heads,),
            in_specs=whole + [own] * 3 + [far] + [both] * len(extra),
            out_specs=out_specs,
        ),
        out_shape=out_shape,
        cost_estimate=pl.CostEstimate(
            flops=cells * 2 * HEAD_DIM * matmuls if split_out else 1000,
            bytes_accessed=2 * rows * width * 2 * (4 + len(extra) + (3 if split_out else 0)) if split_out else 1000,
            transcendentals=cells if split_out else 0,
        ),
        compiler_params=pltpu.CompilerParams(vmem_limit_bytes=48 << 20),
    )(me, ids[:, None], ids[None, :], *owns, fars, *extra)


def dot_f32(a, b, left, right):
    return lax.dot_general(a, b, (((left,), (right,)), ((), ())), preferred_element_type=jnp.float32)


def paired_body(query, key, value, out_weight, lengths, grad_out):
    rows, width = query.shape
    half = width // 2
    groups = lax.axis_size("mp")
    side = groups // 2
    me = lax.axis_index("seq")
    swap = lambda a: lax.ppermute(a, "seq", [(0, 1), (1, 0)])
    first = me == 0
    ends = jnp.cumsum(lengths)
    ids = jnp.concatenate(
        [image_ids(ends, me * rows, rows), image_ids(ends, (1 - me) * rows, rows)]
    )

    def away(a):
        return lax.dynamic_slice_in_dim(a, (1 - me) * half, half, 1)

    fars = swap(jnp.stack([away(query), away(key), away(value)]))
    fars, late_go = lax.optimization_barrier((fars, grad_out))
    far_go = swap(late_go)
    features = out_weight.shape[1]
    weight = out_weight.reshape(side, 2, half, features)
    w_mine = lax.dynamic_index_in_dim(weight, me, 1, keepdims=False).reshape(side * half, features)
    w_away = lax.dynamic_index_in_dim(weight, 1 - me, 1, keepdims=False).reshape(
        side * half, features
    )

    bf = jnp.bfloat16
    cross_own = swap(dot_f32(grad_out, w_away, 1, 1).astype(bf))
    keep_own = dot_f32(grad_out, w_mine, 1, 1).astype(bf)
    cross_far = swap(dot_f32(far_go, w_away, 1, 1).astype(bf))
    keep_far = dot_f32(far_go, w_mine, 1, 1).astype(bf)
    keep = jnp.concatenate([keep_own, keep_far], 0).reshape(2 * rows, side, half)
    got = jnp.concatenate([cross_far, cross_own], 0).reshape(2 * rows, side, half)
    keep, got = keep.transpose(1, 0, 2), got.transpose(1, 0, 2)
    parts = jnp.concatenate([jnp.where(first, keep, got), jnp.where(first, got, keep)], 0)
    d_attention = lax.psum_scatter(
        parts.reshape(groups * 2 * rows, half), "mp", scatter_dimension=0, tiled=True
    )

    owns = (query, key, value)
    where_me = jnp.reshape(me, (1,)).astype(jnp.int32)
    attention = attention_call(forward_kernel, where_me, ids, owns, fars, (), False)
    every = lax.all_gather(attention, "mp", axis=0, tiled=False)
    mine = lax.dynamic_slice_in_dim(every, me * side, side, 0)
    theirs = swap(lax.dynamic_slice_in_dim(every, (1 - me) * side, side, 0))

    def beside(a, b):
        return jnp.stack([jnp.where(first, a, b), jnp.where(first, b, a)], 1)

    mine_own, mine_far = mine[:, :rows], mine[:, rows:]
    their_own, their_far = theirs[:, rows:], theirs[:, :rows]
    att_own = beside(mine_own, their_own)
    att_far = beside(mine_far, their_far)

    def project(att, w):
        return lax.dot_general(
            att,
            w.reshape(side, half, features),
            (((0, 2), (0, 1)), ((), ())),
            preferred_element_type=jnp.float32,
        )

    far_part = project(mine_far, w_mine)
    other = swap((far_part + project(their_far, w_away)).astype(bf))
    mixed = project(mine_own, w_mine) + project(their_own, w_away)
    mixed = (mixed + other.astype(jnp.float32)).astype(bf)
    att_all = jnp.concatenate([att_own, att_far], 2)
    go_all = jnp.concatenate([grad_out, far_go], 0)
    grad_weight = lax.dot_general(
        att_all, go_all, (((2,), (0,)), ((), ())), preferred_element_type=jnp.float32
    ).astype(bf).reshape(out_weight.shape)

    grads = attention_call(
        backward_kernel, where_me, ids, owns, fars, (attention, d_attention), True
    )

    own_grads, got = grads[0], swap(grads[1])

    def home(i):
        own, far = own_grads[i], got[i]
        return jnp.concatenate([jnp.where(first, own, far), jnp.where(first, far, own)], 1)

    grad_query, grad_key, grad_value = home(0), home(1), home(2)
    return (mixed, grad_query, grad_key, grad_value, grad_weight)


def solution(mesh):
    placed = (
        P(("dp", "seq"), "mp"),
        P(("dp", "seq"), "mp"),
        P(("dp", "seq"), "mp"),
        P("seq", "mp"),
        P("dp"),
        P(("dp", "seq"), "mp"),
    )
    heads_here = HEADS_IN_ALL // mesh.shape["mp"]
    paired = mesh.shape["seq"] == 2 and mesh.shape["mp"] % 2 == 0 and heads_here % 2 == 0
    return jax.shard_map(
        paired_body if paired else body,
        mesh=mesh,
        in_specs=placed,
        out_specs=(
            P(("dp", "seq"), "mp"),
            P(("dp", "seq"), "mp"),
            P(("dp", "seq"), "mp"),
            P(("dp", "seq"), "mp"),
            P(("dp", "seq"), "mp"),
        ),
        check_vma=False,
    )
```

```python
import math

import jax
import jax.numpy as jnp
from jax import lax
from jax.experimental import pallas as pl
from jax.experimental.pallas import tpu as pltpu
from jax.sharding import PartitionSpec as P

HEAD_DIM = 128


HEADS_IN_ALL = 32
NEG = -1e30


def image_ids(ends, first, count):
    places = first + jnp.arange(count, dtype=jnp.int32)
    return jnp.sum((places[:, None] >= ends[None, :]).astype(jnp.int32), axis=1)


def body(query, key, value, out_weight, lengths, grad_out):
    tok_rows, width = query.shape
    heads = width // HEAD_DIM
    scale = HEAD_DIM ** (-0.5)
    ends = jnp.cumsum(lengths)
    first_row = lax.axis_index("seq") * tok_rows
    query_ids = image_ids(ends, first_row, tok_rows)
    every_q, every_k, every_v = (
        lax.all_gather(query, "seq", axis=0, tiled=True),
        lax.all_gather(key, "seq", axis=0, tiled=True),
        lax.all_gather(value, "seq", axis=0, tiled=True),
    )
    seq_total = every_k.shape[0]
    block = math.gcd(512, seq_total)
    steps_all = jnp.arange(seq_total // block, dtype=jnp.int32)
    local_q = query.reshape(tok_rows, heads, HEAD_DIM)
    local_k = key.reshape(tok_rows, heads, HEAD_DIM)
    local_v = value.reshape(tok_rows, heads, HEAD_DIM)

    def key_block(index):
        begin = index * block
        keys = lax.dynamic_slice_in_dim(every_k, begin, block, 0).reshape(block, heads, HEAD_DIM)
        vals = lax.dynamic_slice_in_dim(every_v, begin, block, 0).reshape(block, heads, HEAD_DIM)
        return (keys, vals, image_ids(ends, begin, block))

    def masked_scores(left, right, left_ids, right_ids):
        same = left_ids[:, None] == right_ids[None, :]
        score = jnp.einsum("qhd,khd->hqk", left, right, preferred_element_type=jnp.float32) * scale
        return (jnp.where(same[None], score, NEG), same)

    def forward_step(carry, index):
        keys, vals, key_ids = key_block(index)
        top, total, acc = carry
        score, same = masked_scores(local_q, keys, query_ids, key_ids)
        new_top = jnp.maximum(top, jnp.max(score, axis=2))
        weights = jnp.where(same[None], jnp.exp(score - new_top[:, :, None]), 0.0)
        fade = jnp.exp(top - new_top)
        total = total * fade + jnp.sum(weights, axis=2)
        acc = acc * fade[:, :, None] + jnp.einsum(
            "hqk,khd->hqd", weights.astype(jnp.bfloat16), vals, preferred_element_type=jnp.float32
        )
        carry = (new_top, total, acc)
        return (carry, None)

    start_state = (
        jnp.full((heads, tok_rows), NEG, jnp.float32),
        jnp.zeros((heads, tok_rows), jnp.float32),
        jnp.zeros((heads, tok_rows, HEAD_DIM), jnp.float32),
    )
    (top, total, acc), unused = lax.scan(forward_step, start_state, steps_all)
    attn_local = (acc / total[:, :, None]).astype(jnp.bfloat16)
    stats = top + jnp.log(total)
    attention = attn_local.transpose(1, 0, 2).reshape(tok_rows, width)
    every_heads = lax.all_gather(attention, "mp", axis=1, tiled=True)
    weight_full = lax.all_gather(out_weight, "seq", axis=0, tiled=True)
    mixed = jnp.dot(every_heads, weight_full, preferred_element_type=jnp.float32).astype(
        jnp.bfloat16
    )
    rows = weight_full
    d_attention = (
        lax.psum_scatter(
            lax.dot_general(
                rows, grad_out, (((1,), (1,)), ((), ())), preferred_element_type=jnp.float32
            ).astype(jnp.bfloat16),
            "mp",
            scatter_dimension=0,
            tiled=True,
        )
        .astype(jnp.float32)
        .T.astype(jnp.bfloat16)
    )
    token_heads = lax.all_to_all(every_heads, "seq", split_axis=1, concat_axis=0, tiled=True)
    rows = token_heads
    grad_weight = lax.dot_general(
        rows,
        lax.all_gather(grad_out, "seq", axis=0, tiled=True),
        (((0,), (0,)), ((), ())),
        preferred_element_type=jnp.float32,
    ).astype(jnp.bfloat16)
    d_local = d_attention.reshape(tok_rows, heads, HEAD_DIM)
    deltas = jnp.sum(
        d_local.astype(jnp.float32)
        * attention.reshape(tok_rows, heads, HEAD_DIM).astype(jnp.float32),
        axis=2,
    ).T

    def query_step(summed, index):
        keys, vals, key_ids = key_block(index)
        score, same = masked_scores(local_q, keys, query_ids, key_ids)
        prob = jnp.exp(score - stats[:, :, None])
        d_p = jnp.einsum("qhd,khd->hqk", d_local, vals, preferred_element_type=jnp.float32)
        d_score = (prob * (d_p - deltas[:, :, None])).astype(jnp.bfloat16)
        summed = summed + jnp.einsum(
            "hqk,khd->qhd", d_score, keys, preferred_element_type=jnp.float32
        )
        return (summed, None)

    dq_sum, unused = lax.scan(
        query_step, jnp.zeros((tok_rows, heads, HEAD_DIM), jnp.float32), steps_all
    )
    grad_query = (dq_sum * scale).reshape(tok_rows, width).astype(jnp.bfloat16)
    d_piece = lax.all_gather(d_attention.astype(jnp.float32), "seq", axis=0, tiled=True)
    stat_piece = lax.all_gather(stats.T, "seq", axis=0, tiled=True)
    delta_piece = lax.all_gather(deltas.T, "seq", axis=0, tiled=True)
    count = d_piece.shape[0]
    far_q = every_q.reshape(count, heads, HEAD_DIM)
    far_ids = image_ids(ends, jnp.int32(0), count)
    d_far = d_piece.astype(jnp.bfloat16).reshape(count, heads, HEAD_DIM)
    score, same = masked_scores(far_q, local_k, far_ids, query_ids)
    prob = jnp.exp(score - stat_piece.T[:, :, None])
    acc_v = jnp.einsum(
        "hqk,qhd->khd", prob.astype(jnp.bfloat16), d_far, preferred_element_type=jnp.float32
    )
    d_p = jnp.einsum("qhd,khd->hqk", d_far, local_v, preferred_element_type=jnp.float32)
    d_score = (prob * (d_p - delta_piece.T[:, :, None])).astype(jnp.bfloat16)
    acc_k = jnp.einsum("hqk,qhd->khd", d_score, far_q, preferred_element_type=jnp.float32)
    grad_key = (acc_k * scale).reshape(tok_rows, width).astype(jnp.bfloat16)
    grad_value = acc_v.reshape(tok_rows, width).astype(jnp.bfloat16)
    return (mixed, grad_query, grad_key, grad_value, grad_weight)


def masked_softmax(q, k, row_ids, col_ids):
    score = lax.dot_general(q, k, (((1,), (1,)), ((), ())), preferred_element_type=jnp.float32)
    score = score * HEAD_DIM ** (-0.5)
    same = row_ids == col_ids
    score = jnp.where(same, score, NEG)
    top = jnp.max(score, axis=1, keepdims=True)
    weights = jnp.exp(score - top)
    return weights, jnp.sum(weights, axis=1, keepdims=True)


def joined(own, far):
    return jnp.concatenate([own[...], far], axis=0)


def forward_kernel(me, rid, cid, qo, ko, vo, far, out):
    qf, kf, vf = far[0], far[1], far[2]
    weights, total = masked_softmax(joined(qo, qf), joined(ko, kf), rid[...], cid[...])
    acc = jnp.dot(weights.astype(jnp.bfloat16), joined(vo, vf), preferred_element_type=jnp.float32)
    out[...] = (acc / total).astype(jnp.bfloat16)


def prob_kernel(me, rid, cid, qo, ko, far, out):
    weights, total = masked_softmax(joined(qo, far[0]), joined(ko, far[1]), rid[...], cid[...])
    out[0] = weights * (1.0 / total)


def prob_call(me, ids, query, key, fars):
    rows, width = fars.shape[1:]
    heads = width // HEAD_DIM
    own = pl.BlockSpec((rows, HEAD_DIM), lambda h, me: (0, me[0] * heads + h))
    cells = 4 * rows * rows * heads
    return pl.pallas_call(
        prob_kernel,
        grid_spec=pltpu.PrefetchScalarGridSpec(
            num_scalar_prefetch=1,
            grid=(heads,),
            in_specs=[
                pl.BlockSpec((2 * rows, 1), lambda h, me: (0, 0)),
                pl.BlockSpec((1, 2 * rows), lambda h, me: (0, 0)),
                own,
                own,
                pl.BlockSpec((3, rows, HEAD_DIM), lambda h, me: (0, 0, h)),
            ],
            out_specs=pl.BlockSpec((1, 2 * rows, 2 * rows), lambda h, me: (h, 0, 0)),
        ),
        out_shape=jax.ShapeDtypeStruct((heads, 2 * rows, 2 * rows), jnp.float32),
        cost_estimate=pl.CostEstimate(
            flops=cells * 2 * HEAD_DIM, bytes_accessed=cells * 4, transcendentals=cells
        ),
        compiler_params=pltpu.CompilerParams(vmem_limit_bytes=48 << 20),
    )(me, ids[:, None], ids[None, :], query, key, fars)


def backward_kernel(me, rid, cid, qo, ko, vo, far, att, datt, probs, own_out, far_out):
    qf, kf, vf = far[0], far[1], far[2]
    q, k, v = joined(qo, qf), joined(ko, kf), joined(vo, vf)
    d_out = datt[...]
    prob = probs[0]
    delta = jnp.sum(
        d_out.astype(jnp.float32) * att[...].astype(jnp.float32), axis=1, keepdims=True
    )
    d_v = lax.dot_general(
        prob.astype(jnp.bfloat16), d_out, (((0,), (0,)), ((), ())),
        preferred_element_type=jnp.float32,
    )
    d_p = lax.dot_general(d_out, v, (((1,), (1,)), ((), ())), preferred_element_type=jnp.float32)
    d_score = (prob * (d_p - delta)).astype(jnp.bfloat16)
    scale = HEAD_DIM ** (-0.5)
    d_q = jnp.dot(d_score, k, preferred_element_type=jnp.float32) * scale
    d_k = lax.dot_general(
        d_score, q, (((0,), (0,)), ((), ())), preferred_element_type=jnp.float32
    ) * scale
    rows = qo.shape[0]
    for i, grad in enumerate((d_q, d_k, d_v)):
        own_out[i] = grad[:rows].astype(jnp.bfloat16)
        far_out[i] = grad[rows:].astype(jnp.bfloat16)


def attention_call(kernel, me, ids, owns, fars, extra, split_out):
    rows, width = fars.shape[1:]
    heads = width // HEAD_DIM
    own = pl.BlockSpec((rows, HEAD_DIM), lambda h, me: (0, me[0] * heads + h))
    far = pl.BlockSpec((3, rows, HEAD_DIM), lambda h, me: (0, 0, h))
    both = pl.BlockSpec((2 * rows, HEAD_DIM), lambda h, me: (0, h))
    square = pl.BlockSpec((1, 2 * rows, 2 * rows), lambda h, me: (h, 0, 0))
    whole = [
        pl.BlockSpec((2 * rows, 1), lambda h, me: (0, 0)),
        pl.BlockSpec((1, 2 * rows), lambda h, me: (0, 0)),
    ]
    if split_out:
        out_specs = [far] * 2
        out_shape = [jax.ShapeDtypeStruct((3, rows, width), jnp.bfloat16)] * 2
    else:
        out_specs = both
        out_shape = jax.ShapeDtypeStruct((2 * rows, width), jnp.bfloat16)
    matmuls = 5 if split_out else 2
    cells = 4 * rows * rows * heads
    return pl.pallas_call(
        kernel,
        grid_spec=pltpu.PrefetchScalarGridSpec(
            num_scalar_prefetch=1,
            grid=(heads,),
            in_specs=whole + [own] * 3 + [far] + [both, both, square][: len(extra)],
            out_specs=out_specs,
        ),
        out_shape=out_shape,
        cost_estimate=pl.CostEstimate(
            flops=cells * 2 * HEAD_DIM * matmuls if split_out else 1000,
            bytes_accessed=2 * rows * width * 2 * (4 + len(extra) + (3 if split_out else 0)) if split_out else 1000,
            transcendentals=cells if split_out else 0,
        ),
        compiler_params=pltpu.CompilerParams(vmem_limit_bytes=48 << 20),
    )(me, ids[:, None], ids[None, :], *owns, fars, *extra)


def dot_f32(a, b, left, right):
    return lax.dot_general(a, b, (((left,), (right,)), ((), ())), preferred_element_type=jnp.float32)


def paired_body(query, key, value, out_weight, lengths, grad_out):
    rows, width = query.shape
    half = width // 2
    groups = lax.axis_size("mp")
    side = groups // 2
    me = lax.axis_index("seq")
    swap = lambda a: lax.ppermute(a, "seq", [(0, 1), (1, 0)])
    first = me == 0
    ends = jnp.cumsum(lengths)
    ids = jnp.concatenate(
        [image_ids(ends, me * rows, rows), image_ids(ends, (1 - me) * rows, rows)]
    )

    def away(a):
        return lax.dynamic_slice_in_dim(a, (1 - me) * half, half, 1)

    fars = swap(jnp.stack([away(query), away(key), away(value)]))
    fars, late_go = lax.optimization_barrier((fars, grad_out))
    far_go = swap(late_go)
    features = out_weight.shape[1]
    weight = out_weight.reshape(side, 2, half, features)
    w_mine = lax.dynamic_index_in_dim(weight, me, 1, keepdims=False).reshape(side * half, features)
    w_away = lax.dynamic_index_in_dim(weight, 1 - me, 1, keepdims=False).reshape(
        side * half, features
    )

    bf = jnp.bfloat16
    cross_own = swap(dot_f32(grad_out, w_away, 1, 1).astype(bf))
    keep_own = dot_f32(grad_out, w_mine, 1, 1).astype(bf)
    cross_far = swap(dot_f32(far_go, w_away, 1, 1).astype(bf))
    keep_far = dot_f32(far_go, w_mine, 1, 1).astype(bf)
    keep = jnp.concatenate([keep_own, keep_far], 0).reshape(2 * rows, side, half)
    got = jnp.concatenate([cross_far, cross_own], 0).reshape(2 * rows, side, half)
    keep, got = keep.transpose(1, 0, 2), got.transpose(1, 0, 2)
    parts = jnp.concatenate([jnp.where(first, keep, got), jnp.where(first, got, keep)], 0)
    d_attention = lax.psum_scatter(
        parts.reshape(groups * 2 * rows, half), "mp", scatter_dimension=0, tiled=True
    )

    owns = (query, key, value)
    where_me = jnp.reshape(me, (1,)).astype(jnp.int32)
    attention = attention_call(forward_kernel, where_me, ids, owns, fars, (), False)
    every = lax.all_gather(attention, "mp", axis=0, tiled=False)
    mine = lax.dynamic_slice_in_dim(every, me * side, side, 0)
    theirs = swap(lax.dynamic_slice_in_dim(every, (1 - me) * side, side, 0))

    def beside(a, b):
        return jnp.stack([jnp.where(first, a, b), jnp.where(first, b, a)], 1)

    mine_own, mine_far = mine[:, :rows], mine[:, rows:]
    their_own, their_far = theirs[:, rows:], theirs[:, :rows]
    att_own = beside(mine_own, their_own)
    att_far = beside(mine_far, their_far)

    def project(att, w):
        return lax.dot_general(
            att,
            w.reshape(side, half, features),
            (((0, 2), (0, 1)), ((), ())),
            preferred_element_type=jnp.float32,
        )

    far_part = project(mine_far, w_mine)
    other = swap((far_part + project(their_far, w_away)).astype(bf))
    mixed = project(mine_own, w_mine) + project(their_own, w_away)
    mixed = (mixed + other.astype(jnp.float32)).astype(bf)
    att_all = jnp.concatenate([att_own, att_far], 2)
    go_all = jnp.concatenate([grad_out, far_go], 0)
    grad_weight = lax.dot_general(
        att_all, go_all, (((2,), (0,)), ((), ())), preferred_element_type=jnp.float32
    ).astype(bf).reshape(out_weight.shape)

    probs = prob_call(where_me, ids, query, key, fars)
    grads = attention_call(
        backward_kernel, where_me, ids, owns, fars, (attention, d_attention, probs), True
    )

    own_grads, got = grads[0], swap(grads[1])

    def home(i):
        own, far = own_grads[i], got[i]
        return jnp.concatenate([jnp.where(first, own, far), jnp.where(first, far, own)], 1)

    grad_query, grad_key, grad_value = home(0), home(1), home(2)
    return (mixed, grad_query, grad_key, grad_value, grad_weight)


def solution(mesh):
    placed = (
        P(("dp", "seq"), "mp"),
        P(("dp", "seq"), "mp"),
        P(("dp", "seq"), "mp"),
        P("seq", "mp"),
        P("dp"),
        P(("dp", "seq"), "mp"),
    )
    heads_here = HEADS_IN_ALL // mesh.shape["mp"]
    paired = mesh.shape["seq"] == 2 and mesh.shape["mp"] % 2 == 0 and heads_here % 2 == 0
    return jax.shard_map(
        paired_body if paired else body,
        mesh=mesh,
        in_specs=placed,
        out_specs=(
            P(("dp", "seq"), "mp"),
            P(("dp", "seq"), "mp"),
            P(("dp", "seq"), "mp"),
            P(("dp", "seq"), "mp"),
            P(("dp", "seq"), "mp"),
        ),
        check_vma=False,
    )
```
